256 devices in a mesh: replica: 8 (over x, z_lo), fsdp: 32 (over y, z_hi, core).
Axes of the slice: x: 4, y: 4, z: 8 (z_hi: 4, z_lo: 2; z = z_hi * 2 + z_lo), core: 2. Of those that a mesh axis runs over, the one named last changes fastest.
Arguments:
- tokens: bfloat16 [2, 131072, 4096], P(None, ('replica', 'fsdp')), may hold values from -6 to 6
- targets: bfloat16 [2, 131072, 512], P(None, ('replica', 'fsdp')), may hold values from -6 to 6
- work_weights: float32 [8, 4096, 512], P('replica', 'fsdp'), may hold values from -6 to 6
- adam_first: float32 [8, 4096, 512], P('replica', 'fsdp'), may hold values from -0.001953125 to 0.001953125
- adam_second: float32 [8, 4096, 512], P('replica', 'fsdp'), may hold values from 7.450581e-09 to 1.1920929e-07
- anchor: float32 [4096, 512], P('fsdp'), may hold values from -6 to 6
- momentum: float32 [4096, 512], P('fsdp'), may hold values from -6 to 6
Outputs:
- new_weights: float32 [8, 4096, 512], P('replica', 'fsdp')
- new_anchor: float32 [4096, 512], P('fsdp')
- new_momentum: float32 [4096, 512], P('fsdp')
The draws below stay inside these ranges and needn't reach their ends.
All inputs are finite; a program needn't handle non-finite values.
Results may differ from the reference program's by a relative error of at most 0.0004.
Values may be sent and summed in bfloat16 or wider, within the bound.
No kernel may reach another device: no remote copies, remote signals or barrier semaphores. Data moves between devices by JAX's collectives and lax.ppermute only.
A program may use at most 64 MiB of HBM per device.

```python
import math
import jax
import jax.numpy as jnp

D = 4096
INNER = 2
TOK_DEV = 512
KVW = 512
ROWS = 131072
N_REPLICA = 8
N_FSDP = 32


def steps_of(own_key, shape, pieces, smallest, high):
    level = 1.0
    for position, parts in pieces:
        steps = jax.random.uniform(jax.random.fold_in(jax.random.fold_in(own_key, 6), position), (parts,), jnp.float32, smallest / len(pieces), high / len(pieces))
        level = level * jnp.repeat(jnp.exp(steps), shape[position] // parts).reshape((-1,) + (1,) * (len(shape) - 1 - position))
    return level


def scatter_about(key, dims, scale, bound, split=(), kind=jnp.bfloat16):
    entries = scale * jax.random.normal(key, dims, jnp.float32)
    if split:
        entries = entries * steps_of(key, dims, split, -0.22, 0.18)
    return jnp.clip(entries, -bound, bound).astype(kind)


def setup_inputs(seed: int = 0) -> dict:
    streams_of = jax.random.split(jax.random.key(seed), 8)
    return {
        "tokens": scatter_about(streams_of[0], (INNER, ROWS, D), 1.0, 6.0, ((1, 256),)),
        "targets": scatter_about(streams_of[1], (INNER, ROWS, KVW), 1.0, 6.0, ((1, 256),)),
        "work_weights": scatter_about(streams_of[2], (N_REPLICA, D, KVW), 1.0, 6.0, ((0, 8), (1, 32)), jnp.float32),
        "adam_first": scatter_about(streams_of[3], (N_REPLICA, D, KVW), (1.0 / (TOK_DEV * N_FSDP * D) ** 0.5), 0.001953125, ((0, 8), (1, 32)), jnp.float32),
        "adam_second": jnp.clip(jnp.exp(math.log(1.1920928955078125e-07) - 2.7725887 * jax.random.uniform(streams_of[4], (N_REPLICA, D, KVW), jnp.float32) ** steps_of(streams_of[4], (N_REPLICA, D, KVW), ((0, 8), (1, 32)), -0.2, 0.2)), 7.450580596923828e-09, 1.1920928955078125e-07),
        "anchor": scatter_about(streams_of[5], (D, KVW), 1.0, 6.0, ((0, 32),), jnp.float32),
        "momentum": scatter_about(streams_of[6], (D, KVW), 0.5, 6.0, ((0, 32),), jnp.float32),
    }


OUTER_MU = 0.9
OUTER_RATE = 0.7
INNER_RATE = 0.05
BETA_ONE = 0.9
BETA_TWO = 0.95
EPSILON = 1e-08
DECAY = 0.1
MIXING = 0.5

def reference(tokens, targets, work_weights, adam_first, adam_second, anchor, momentum):
    row_count = TOK_DEV * N_FSDP
    scale = float(D) ** (-0.5)
    total = jnp.zeros(anchor.shape, jnp.float32)
    for replica in range(N_REPLICA):
        total = total + (anchor - work_weights[replica])
    outer_mean = total / N_REPLICA
    new_momentum = OUTER_MU * momentum + outer_mean
    new_anchor = anchor - OUTER_RATE * (outer_mean + OUTER_MU * new_momentum)
    results = []
    for replica in range(N_REPLICA):
        weights = work_weights[replica]
        first = adam_first[replica]
        second = adam_second[replica]
        for step in range(INNER):
            inputs = tokens[step, replica * row_count:(replica + 1) * row_count]
            wanted = targets[step, replica * row_count:(replica + 1) * row_count]
            keys = jnp.dot(inputs, weights.astype(jnp.bfloat16), preferred_element_type=jnp.float32) * scale
            slope = ((keys - wanted.astype(jnp.float32)) / row_count).astype(jnp.bfloat16)
            grad = jnp.dot(inputs.T, slope, preferred_element_type=jnp.float32) * scale
            first = BETA_ONE * first + (1.0 - BETA_ONE) * grad
            second = BETA_TWO * second + (1.0 - BETA_TWO) * grad * grad
            weights = weights - INNER_RATE * (first / (jnp.sqrt(second) + EPSILON) + DECAY * weights)
            if step == 0:
                weights = MIXING * weights + (1.0 - MIXING) * new_anchor
        results.append(weights)
    return (jnp.stack(results), new_anchor, new_momentum)
```

```python
import functools

import jax
import jax.numpy as jnp
from jax import lax
from jax.experimental import pallas as pl
from jax.experimental.pallas import tpu as pltpu
from jax.sharding import PartitionSpec as P

OUTER_MU = 0.9
OUTER_RATE = 0.7
INNER_RATE = 0.05
BETA_ONE = 0.9
BETA_TWO = 0.95
EPSILON = 1e-08
DECAY = 0.1
MIXING = 0.5

MIB = 1024 * 1024
CHUNKS = ((128, "zy"), (128, "zy"))
STEPS = {"y": (0, 1, 3, 2), "z": (0, 1, 3, 2)}
SHIFTS = {"y": 3, "z": 1}


def swap(array, axis, mask):
    count = lax.axis_size(axis)
    return lax.ppermute(array, axis, [(i, i ^ mask) for i in range(count)])


def swap_core(array):
    return swap(array, "fsdp", 1)


def swap_all(arrays, axis):
    return [swap(a, "fsdp", k << SHIFTS[axis]) for a, k in zip(arrays, STEPS[axis][1:])]


def block_at(place, route, i, j):
    steps = {route[1]: STEPS[route[1]][i], route[0]: STEPS[route[0]][j]}
    index = (place[0] ^ steps["y"]) * 4 + (place[1] ^ steps["z"])
    return pl.ds(pl.multiple_of(index * 256, 256), 256)


def step_kernel(step, width, route, scale, row_count, place, own, peer, target, *rest):
    gathered, outs = rest[:4], rest[4:8]
    tokens, weights, slope, sems = rest[8:]
    copies = []
    for i in range(4):
        columns = slice(i * 1024, i * 1024 + 1024)
        for part, source in enumerate((own, peer)):
            copy = pltpu.make_async_copy(
                source.at[step, :, columns], tokens.at[part * 512 : part * 512 + 512, columns], sems.at[i, part]
            )
            copy.start()
            copies.append(copy)
    for i in range(4):
        for j in range(4):
            weights[:, block_at(place, route, i, j)] = gathered[i][j * width : (j + 1) * width, :]
    total = None
    for i in range(4):
        copies[2 * i].wait()
        copies[2 * i + 1].wait()
        columns = slice(i * 1024, i * 1024 + 1024)
        product = lax.dot_general(
            weights[:, columns], tokens[:, columns], (((1,), (1,)), ((), ())), preferred_element_type=jnp.float32
        )
        total = product if total is None else total + product
    slope[...] = ((total * scale - target[...].astype(jnp.float32)) / row_count).astype(jnp.bfloat16)
    for i in range(4):
        for j in range(4):
            product = jnp.dot(
                slope[...], tokens[:, block_at(place, route, i, j)], preferred_element_type=jnp.float32
            )
            outs[i][j * width : (j + 1) * width, :] = (product * scale).astype(jnp.bfloat16)


def step_call(step, route, place, tokens, peer_tokens, target, gathered, scale, row_count):
    vmem = pl.BlockSpec(memory_space=pltpu.VMEM)
    hbm = pl.BlockSpec(memory_space=pltpu.HBM)
    width = target.shape[0]
    return pl.pallas_call(
        functools.partial(step_kernel, step, width, route, scale, row_count),
        in_specs=[pl.BlockSpec(memory_space=pltpu.SMEM), hbm, hbm] + [vmem] * 5,
        out_specs=[vmem] * 4,
        out_shape=[jax.ShapeDtypeStruct((4 * width, 256), jnp.bfloat16)] * 4,
        scratch_shapes=[
            pltpu.VMEM((1024, 4096), jnp.bfloat16),
            pltpu.VMEM((width, 4096), jnp.bfloat16),
            pltpu.VMEM((width, 1024), jnp.bfloat16),
            pltpu.SemaphoreType.DMA((4, 2)),
        ],
        compiler_params=pltpu.CompilerParams(vmem_limit_bytes=32 * MIB),
        cost_estimate=pl.CostEstimate(flops=4 * 1024 * 4096 * width, bytes_accessed=12 * MIB, transcendentals=0),
        name="step",
    )(place, tokens, peer_tokens, target, *gathered)


def small_call(kernel, shapes, *args, smem=0):
    vmem = pl.BlockSpec(memory_space=pltpu.VMEM)
    return pl.pallas_call(
        kernel,
        in_specs=[pl.BlockSpec(memory_space=pltpu.SMEM)] * smem + [vmem] * (len(args) - smem),
        out_specs=[vmem] * len(shapes),
        out_shape=[jax.ShapeDtypeStruct(*s) for s in shapes],
        compiler_params=pltpu.CompilerParams(vmem_limit_bytes=16 * MIB),
        name=kernel.__name__,
    )(*args)


def total_of(blocks):
    total = blocks[0][...].astype(jnp.float32)
    for block in blocks[1:]:
        total = total + block[...].astype(jnp.float32)
    return total


def split_kernel(*refs):
    width = refs[0].shape[0] // 4
    for j, out in enumerate(refs[4:]):
        rows = slice(j * width, j * width + width)
        out[...] = total_of([ref.at[rows] for ref in refs[:4]]).astype(out.dtype)


def adam(grad, weights, first, second):
    first = BETA_ONE * first + (1.0 - BETA_ONE) * grad
    second = BETA_TWO * second + (1.0 - BETA_TWO) * grad * grad
    weights = weights - INNER_RATE * (first / (jnp.sqrt(second) + EPSILON) + DECAY * weights)
    return weights, first, second


def update_kernel(a, b, c, d, weights, first, second, anchor, weights_out, first_out, second_out, low_out):
    new, m, v = adam(total_of((a, b, c, d)), weights[...], first[...], second[...])
    new = MIXING * new + (1.0 - MIXING) * anchor[...]
    weights_out[...] = new
    first_out[...] = m
    second_out[...] = v
    low_out[...] = new.astype(jnp.bfloat16)


def last_kernel(place, a, b, c, d, weights, first, second, keep, send):
    new, _, _ = adam(total_of((a, b, c, d)), weights[...], first[...], second[...])
    core = place[2]
    keep[...] = jnp.where(core == 0, new[:, :128], new[:, 128:])
    send[...] = jnp.where(core == 0, new[:, 128:], new[:, :128])


def gather(block, route):
    blocks = jnp.concatenate([block] + swap_all([block] * 3, route[0]), axis=0)
    return [blocks] + swap_all([blocks] * 3, route[1])


def scatter(parts, route):
    width = parts[0].shape[0] // 4
    parts = [parts[0]] + swap_all(parts[1:], route[1])
    block = (width, 256)
    shapes = [(block, jnp.float32)] + [(block, jnp.bfloat16)] * 3
    parts = small_call(split_kernel, shapes, *parts)
    return [parts[0]] + swap_all(parts[1:], route[0])


def shards(tokens, targets, work_weights, adam_first, adam_second, anchor, momentum):
    device = lax.axis_index("fsdp")
    core = device % 2
    place = jnp.stack([device // 8, (device // 2) % 4, core]).astype(jnp.int32)
    scale = float(tokens.shape[2]) ** (-0.5)
    row_count = tokens.shape[1] * lax.axis_size("fsdp")

    def mine(array):
        return jnp.where(core == 0, array[..., :256], array[..., 256:])

    def theirs(array):
        return jnp.where(core == 0, array[..., 256:], array[..., :256])

    def across(array):
        own = jnp.swapaxes(mine(array), -1, -2)
        other = swap_core(jnp.swapaxes(theirs(array), -1, -2))
        return jnp.where(
            core == 0, jnp.concatenate([own, other], -1), jnp.concatenate([other, own], -1)
        )

    edges = [0]
    for width, _ in CHUNKS:
        edges.append(edges[-1] + width)
    cuts = [slice(a, b) for a, b in zip(edges[:-1], edges[1:])]
    routes = [route for _, route in CHUNKS]

    weights, first, second = work_weights[0], adam_first[0], adam_second[0]
    block = across(weights.astype(jnp.bfloat16))
    block, tokens, targets, first, second, weights, anchor, momentum = lax.optimization_barrier(
        (block, tokens, targets, first, second, weights, anchor, momentum)
    )
    peer_tokens = swap_core(tokens)
    lows = [block[cut] for cut in cuts]
    gathered = [gather(low, route) for low, route in zip(lows, routes)]
    own = jnp.swapaxes(mine(targets), -1, -2)
    target = jnp.concatenate([own, swap_core(jnp.swapaxes(theirs(targets), -1, -2))], axis=-1)
    state = across(jnp.stack([weights, first, second]))
    delta = anchor - weights
    for mask in (2, 6):
        delta = delta + swap(delta, "replica", mask)

    def run(step, gathered):
        return [
            list(step_call(step, route, place, tokens, peer_tokens, target[step, cut], pieces, scale, row_count))
            for route, cut, pieces in zip(routes, cuts, gathered)
        ]

    grads = run(0, gathered)
    first_part, delta = lax.optimization_barrier((grads[0][0], delta))
    grads[0] = [first_part] + grads[0][1:]
    outer_mean = (delta + swap(delta, "replica", 1)) / lax.axis_size("replica")
    new_momentum = OUTER_MU * momentum + outer_mean
    new_anchor = anchor - OUTER_RATE * (outer_mean + OUTER_MU * new_momentum)
    anchor_part = across(new_anchor)

    states, gathered = [], []
    for (width, route), cut, parts in zip(CHUNKS, cuts, grads):
        shape = (width, 256)
        *new_state, low = small_call(
            update_kernel, [(shape, jnp.float32)] * 3 + [(shape, jnp.bfloat16)],
            *scatter(parts, route), state[0, cut], state[1, cut], state[2, cut], anchor_part[cut],
        )
        states.append(new_state)
        gathered.append(gather(low, route))
    grads = run(1, gathered)
    keeps, sends = [], []
    for (width, route), parts, new_state in zip(CHUNKS, grads, states):
        keep, send = small_call(
            last_kernel, [((width, 128), jnp.float32)] * 2, place, *scatter(parts, route), *new_state, smem=1
        )
        keeps.append(keep)
        sends.append(swap_core(send))
    keep, send = jnp.concatenate(keeps, 0), jnp.concatenate(sends, 0)
    new_weights = jnp.where(core == 0, jnp.concatenate([keep, send], 0), jnp.concatenate([send, keep], 0)).T
    return (new_weights[None], new_anchor, new_momentum)


def solution(mesh):
    return jax.shard_map(
        shards,
        mesh=mesh,
        in_specs=(
            P(None, ("replica", "fsdp"), None),
            P(None, ("replica", "fsdp"), None),
            P("replica", "fsdp", None),
            P("replica", "fsdp", None),
            P("replica", "fsdp", None),
            P("fsdp", None),
            P("fsdp", None),
        ),
        out_specs=(P("replica", "fsdp", None), P("fsdp", None), P("fsdp", None)),
        check_vma=False,
    )
```

```python
import functools

import jax
import jax.numpy as jnp
from jax import lax
from jax.experimental import pallas as pl
from jax.experimental.pallas import tpu as pltpu
from jax.sharding import PartitionSpec as P

OUTER_MU = 0.9
OUTER_RATE = 0.7
INNER_RATE = 0.05
BETA_ONE = 0.9
BETA_TWO = 0.95
EPSILON = 1e-08
DECAY = 0.1
MIXING = 0.5

MIB = 1024 * 1024
WIDTHS = (128, 128)
CUTS = (slice(0, WIDTHS[0]), slice(WIDTHS[0], WIDTHS[0] + WIDTHS[1]))
STEPS = (0, 1, 3, 2)
SHIFTS = {"y": 3, "z": 1}
TIE_SUMS = 0
TIE_GATHER = 0


def swap(array, axis, mask):
    count = lax.axis_size(axis)
    return lax.ppermute(array, axis, [(i, i ^ mask) for i in range(count)])


def swap_core(array):
    return swap(array, "fsdp", 1)


def swap_all(arrays, axis):
    return [swap(a, "fsdp", k << SHIFTS[axis]) for a, k in zip(arrays, STEPS[1:])]


def block_at(place, i, j):
    index = (place[0] ^ STEPS[i]) * 4 + (place[1] ^ STEPS[j])
    return pl.ds(pl.multiple_of(index * 256, 256), 256)


def call(kernel, shapes, *args, smem=0, hbm=0, scratch=(), limit=16, cost=None, name=None):
    vmem = pl.BlockSpec(memory_space=pltpu.VMEM)
    specs = [pl.BlockSpec(memory_space=pltpu.SMEM)] * smem + [pl.BlockSpec(memory_space=pltpu.HBM)] * hbm
    return pl.pallas_call(
        kernel,
        in_specs=specs + [vmem] * (len(args) - smem - hbm),
        out_specs=[vmem] * len(shapes),
        out_shape=[jax.ShapeDtypeStruct(*s) for s in shapes],
        scratch_shapes=scratch,
        compiler_params=pltpu.CompilerParams(vmem_limit_bytes=limit * MIB),
        cost_estimate=cost,
        name=name or kernel.__name__,
    )(*args)


def load_kernel(step, own, peer, tokens, sems):
    copies = [
        pltpu.make_async_copy(source.at[step], tokens.at[part * 512 : part * 512 + 512], sems.at[part])
        for part, source in enumerate((own, peer))
    ]
    for copy in copies:
        copy.start()
    for copy in copies:
        copy.wait()


def load_call(step, tokens, peer_tokens):
    (held,) = call(
        functools.partial(load_kernel, step), [((1024, 4096), jnp.bfloat16)],
        pltpu.with_memory_space_constraint(tokens, pltpu.HBM), peer_tokens, hbm=2, limit=16,
        scratch=[pltpu.SemaphoreType.DMA((2,))],
        cost=pl.CostEstimate(flops=0, bytes_accessed=16 * MIB, transcendentals=0), name="load_tokens",
    )
    return held


def chunk_kernel(step, cut, scale, row_count, place, tokens, own_target, peer_target, *rest):
    gathered, outs, weights = rest[:4], rest[4:8], rest[8]
    width = weights.shape[0]
    for i in range(4):
        for j in range(4):
            weights[:, block_at(place, i, j)] = gathered[i][j * width : (j + 1) * width, :]
    total = None
    for i in range(4):
        columns = slice(i * 1024, i * 1024 + 1024)
        product = lax.dot_general(
            weights[:, columns], tokens[:, columns], (((1,), (1,)), ((), ())), preferred_element_type=jnp.float32
        )
        total = product if total is None else total + product
    target = jnp.concatenate([own_target[step, cut, :], peer_target[step, cut, :]], axis=1)
    slope = ((total * scale - target.astype(jnp.float32)) / row_count).astype(jnp.bfloat16)
    for i in range(4):
        for j in range(4):
            product = jnp.dot(slope, tokens[:, block_at(place, i, j)], preferred_element_type=jnp.float32)
            outs[i][j * width : (j + 1) * width, :] = (product * scale).astype(jnp.bfloat16)


def chunk_call(step, chunk, place, held, target, gathered, scale, row_count):
    width = WIDTHS[chunk]
    return call(
        functools.partial(chunk_kernel, step, CUTS[chunk], scale, row_count),
        [((4 * width, 256), jnp.bfloat16)] * 4,
        place, held, *target, *gathered, smem=1, limit=16,
        scratch=[pltpu.VMEM((width, 4096), jnp.bfloat16)],
        cost=pl.CostEstimate(flops=4 * 1024 * 4096 * width, bytes_accessed=12 * MIB, transcendentals=0),
        name="chunk",
    )


def total_of(blocks):
    total = blocks[0][...].astype(jnp.float32)
    for block in blocks[1:]:
        total = total + block[...].astype(jnp.float32)
    return total


def part_of(refs, width, j):
    rows = slice(j * width, (j + 1) * width)
    return total_of([ref.at[rows] for ref in refs])


def halves(core, array):
    low, high = array[:, :256], array[:, 256:]
    return jnp.where(core == 0, low, high), jnp.where(core == 0, high, low)


def joined(core, own, other, axis=1):
    return jnp.where(core == 0, jnp.concatenate([own, other], axis), jnp.concatenate([other, own], axis))


def low_kernel(place, weights, mine, theirs):
    own, other = halves(place[2], weights[...])
    mine[...] = own.T.astype(jnp.bfloat16)
    theirs[...] = other.T.astype(jnp.bfloat16)


def state_kernel(place, weights, first, second, mine, theirs):
    for i, ref in enumerate((weights, first, second)):
        own, other = halves(place[2], ref[...])
        mine[i] = own.T
        theirs[i] = other.T


def target_kernel(place, targets, mine, theirs):
    for i in range(2):
        own, other = halves(place[2], targets[i])
        mine[i] = own.astype(jnp.float32).T.astype(jnp.bfloat16)
        theirs[i] = other.astype(jnp.float32).T.astype(jnp.bfloat16)


def outer_kernel(replicas, place, anchor, momentum, delta, other_delta, new_anchor, new_momentum, mine, theirs):
    mean = (delta[...] + other_delta[...]) / replicas
    moved = OUTER_MU * momentum[...] + mean
    new = anchor[...] - OUTER_RATE * (mean + OUTER_MU * moved)
    new_anchor[...] = new
    new_momentum[...] = moved
    own, other = halves(place[2], new)
    mine[...] = own.T
    theirs[...] = other.T


def split_kernel(*refs):
    for j, out in enumerate(refs[4:]):
        out[...] = part_of(refs[:4], out.shape[0], j).astype(out.dtype)


def adam(grad, weights, first, second):
    first = BETA_ONE * first + (1.0 - BETA_ONE) * grad
    second = BETA_TWO * second + (1.0 - BETA_TWO) * grad * grad
    weights = weights - INNER_RATE * (first / (jnp.sqrt(second) + EPSILON) + DECAY * weights)
    return weights, first, second


def update(place, cut, grad, state, other_state, anchor, other_anchor, outs):
    core = place[2]
    weights, first, second = [joined(core, state[i, cut, :], other_state[i, cut, :]) for i in range(3)]
    new, m, v = adam(grad, weights, first, second)
    new = MIXING * new + (1.0 - MIXING) * joined(core, anchor[cut, :], other_anchor[cut, :])
    for out, value in zip(outs, (new, m, v)):
        out[...] = value
    return new.astype(jnp.bfloat16)


def update_kernel(cut, place, *refs):
    sums, state, outs, low = refs[:4], refs[4:8], refs[8:11], refs[11]
    low[...] = update(place, cut, total_of(sums), *state, outs)


def last_kernel(place, a, b, c, d, weights, first, second, keep, send):
    new, _, _ = adam(total_of((a, b, c, d)), weights[...], first[...], second[...])
    core = place[2]
    keep[...] = jnp.where(core == 0, new[:, :128], new[:, 128:])
    send[...] = jnp.where(core == 0, new[:, 128:], new[:, :128])


def final_kernel(place, keep_a, keep_b, got_a, got_b, out):
    own = jnp.concatenate([keep_a[...], keep_b[...]], axis=0)
    other = jnp.concatenate([got_a[...], got_b[...]], axis=0)
    out[...] = joined(place[2], own, other, 0).T


def gather_y(blocks):
    blocks = jnp.concatenate(blocks, axis=0)
    return [blocks] + swap_all([blocks] * 3, "y")


def after(values, *others):
    return list(lax.optimization_barrier((*values, *others))[: len(values)])


def sum_y(parts):
    block = (parts[0].shape[0] // 4, 256)
    return call(split_kernel, [(block, jnp.float32)] + [(block, jnp.bfloat16)] * 3, *parts)


def shards(tokens, targets, work_weights, adam_first, adam_second, anchor, momentum):
    device = lax.axis_index("fsdp")
    core = device % 2
    place = jnp.stack([device // 8, (device // 2) % 4, core]).astype(jnp.int32)
    scale = float(tokens.shape[2]) ** (-0.5)
    row_count = tokens.shape[1] * lax.axis_size("fsdp")
    weights, first, second = work_weights[0], adam_first[0], adam_second[0]
    f32, b16 = jnp.float32, jnp.bfloat16

    mine, theirs = call(low_kernel, [((256, 128), b16)] * 2, place, weights, smem=1)
    block = joined(core, mine, swap_core(theirs))
    block, tokens, targets = lax.optimization_barrier((block, tokens, targets))
    far = [block] + swap_all([block] * 3, "z")
    peer_tokens = swap_core(tokens)
    *far, peer_tokens = lax.optimization_barrier((*far, peer_tokens))
    gathered = [gather_y([b[cut] for b in far]) for cut in CUTS]

    own_target, other = call(target_kernel, [((2, 256, 512), b16)] * 2, place, targets, smem=1)
    target = (own_target, swap_core(other))
    state, other = call(state_kernel, [((3, 256, 128), f32)] * 2, place, weights, first, second, smem=1)
    other_state = swap_core(other)
    delta = anchor - weights
    for mask in (2, 6):
        delta = delta + swap(delta, "replica", mask)

    def run(step, held, gathered):
        sums = []
        for chunk in range(2):
            parts = chunk_call(step, chunk, place, held, target, gathered[chunk], scale, row_count)
            sums.append([parts[0]] + swap_all(parts[1:], "y"))
        return sums

    parts, more = run(0, load_call(0, tokens, peer_tokens), gathered)
    first_part, delta = lax.optimization_barrier((parts[0], delta))
    parts[0] = first_part
    new_anchor, new_momentum, own_anchor, other = call(
        functools.partial(outer_kernel, lax.axis_size("replica")), [((128, 512), f32)] * 2 + [((256, 128), f32)] * 2,
        place, anchor, momentum, delta, swap(delta, "replica", 1), smem=1, name="outer_update",
    )
    held_state = (state, other_state, own_anchor, swap_core(other))

    states, gathered, chunks = [], [], []
    for chunk, parts in enumerate((parts, more)):
        own, *others = sum_y(parts)
        if TIE_SUMS and chunk == 1:
            others = after(others, chunks[0][TIE_SUMS])
        shapes = [((WIDTHS[chunk], 256), f32)] * 3 + [((WIDTHS[chunk], 256), b16)]
        *new_state, low = call(
            functools.partial(update_kernel, CUTS[chunk]), shapes,
            place, own, *swap_all(others, "z"), *held_state, smem=1, name="update",
        )
        states.append(new_state)
        chunks.append([low] + swap_all([low] * 3, "z"))
    gathered.append(gather_y(chunks[0]))
    blocks = chunks[1]
    if TIE_GATHER:
        blocks = after(blocks, *gathered[0][1 : 1 + TIE_GATHER])
    gathered.append(gather_y(blocks))
    held = load_call(1, tokens, peer_tokens)
    keeps, gots = [], []
    for parts, state, width in zip(run(1, held, gathered), states, WIDTHS):
        own, *others = sum_y(parts)
        keep, send = call(last_kernel, [((width, 128), f32)] * 2, place, own, *swap_all(others, "z"), *state, smem=1)
        keeps.append(keep)
        gots.append(swap_core(send))
    (new_weights,) = call(final_kernel, [((128, 512), f32)], place, *keeps, *gots, smem=1)
    return (new_weights[None], new_anchor, new_momentum)


def solution(mesh):
    return jax.shard_map(
        shards,
        mesh=mesh,
        in_specs=(
            P(None, ("replica", "fsdp"), None),
            P(None, ("replica", "fsdp"), None),
            P("replica", "fsdp", None),
            P("replica", "fsdp", None),
            P("replica", "fsdp", None),
            P("fsdp", None),
            P("fsdp", None),
        ),
        out_specs=(P("replica", "fsdp", None), P("fsdp", None), P("fsdp", None)),
        check_vma=False,
    )
```
